32 devices in a mesh: group: 2 (over y), wide: 4 (over z), narrow: 2 (over x), sub: 2 (over core).
Axes of the slice: x: 2, y: 2, z: 4, core: 2. Of those that a mesh axis runs over, the one named last changes fastest.
Arguments:
- amplitudes: bfloat16 [64, 2048, 2048], P(('group', 'wide'), None, ('narrow', 'sub')), parts along dimension 0, may hold values from -6 to 6
- t_mask: int32 [64, 32, 32], P(('group', 'wide'), None, ('narrow', 'sub')), parts along dimension 0, may hold values 0 or 1
- integrals: bfloat16 [4, 2048, 2048], P('group', 'narrow', 'sub'), parts along dimension 0, may hold values from -0.09375 to 0.09375
- w_mask: int32 [4, 32, 32], P('group', 'narrow', 'sub'), parts along dimension 0, may hold values 0 or 1
- owner_map: int32 [32], replicated, may hold values from 0 to 31, each once
Outputs:
- residual: bfloat16 [32, 2048, 2048], P(('group', 'narrow'), 'wide', 'sub'), parts along dimension 0
The draws below stay inside these ranges and needn't reach their ends.
There are 2 independent parts, one for each index of `group`. The reference program is written for one: setup_inputs(seed, part) draws one part's arguments, and reference() takes and returns one part's arrays. A program takes and returns all parts, laid end to end along the dimension named above; an argument that names none is the same for every part. Nothing has to cross between parts.
Inputs may be any that keep to these rules, and one draw needn't show every extreme that they name: `owner_map`: each virtual tile appears exactly once.
All inputs are finite; a program needn't handle non-finite values. No bound on the sum of `t_mask` or of `w_mask` on one device may be relied on, other than what follows from the above.
Results may differ from the reference program's by a relative error of at most 0.0052.
Values may be sent and summed in bfloat16 or wider, within the bound.
No kernel may reach another device: no remote copies, remote signals or barrier semaphores. Data moves between devices by JAX's collectives and lax.ppermute only.
A program may use at most 320 MiB of HBM per device.

```python
import jax
import jax.numpy as jnp
from jax import lax

K_OCC = 2
TILE = 64
VTILES = 32
I_OCC = 16
PAIRS = 32
VIRT = 2048
N_NARROW = 2


def place_ends(entries, stream_key, smallest, largest):
    index_at = [jax.random.randint(jax.random.fold_in(stream_key, axis), (), 0, length) for axis, length in enumerate(entries.shape)]
    main_axis = entries.shape.index(max(entries.shape))
    beside = index_at[:main_axis] + [(index_at[main_axis] + 1) % entries.shape[main_axis]] + index_at[main_axis + 1:]
    return entries.at[tuple(index_at)].set(smallest).at[tuple(beside)].set(largest)


def block_levels(rng, shape, split, low, largest):
    factor_of, own = 1.0, jax.random.fold_in(rng, 6)
    for dim, blocks in split:
        steps = jnp.exp(jax.random.uniform(jax.random.fold_in(own, dim), (blocks,), jnp.float32, low / len(split), largest / len(split)))
        factor_of = factor_of * jnp.repeat(steps, shape[dim] // blocks).reshape([-1 if axis == dim else 1 for axis in range(len(shape))])
    return factor_of


def scatter_about(key, extent, width, reach, cuts=(), dtype=jnp.bfloat16):
    drawn = jax.random.normal(key, extent, jnp.float32) * width
    if len(cuts) > 0:
        drawn = block_levels(key, extent, cuts, -0.22, 0.18) * drawn
    return jnp.clip(drawn, min=-reach, max=reach).astype(dtype)


def setup_inputs(seed: int = 0, part: int = 0) -> dict:
    streams_of = jax.random.split(jax.random.key(seed), 6)
    part_splits = jax.random.split(jax.random.fold_in(streams_of[5], part), 6)
    amplitudes = scatter_about(part_splits[0], (PAIRS, VIRT, VIRT), 1.0, 6.0, ((0, 4), (2, 4)))
    t_mask = place_ends((jax.random.randint(part_splits[1], (PAIRS, VTILES, VTILES), 0, 4) < 3).astype(jnp.int32), jax.random.fold_in(part_splits[1], 1), 0, 1)
    integrals = scatter_about(part_splits[2], (K_OCC, VIRT, VIRT), (K_OCC * VIRT) ** -0.5, 0.09375, ((1, 2), (2, 2)))
    w_mask = place_ends((jax.random.randint(part_splits[3], (K_OCC, VTILES, VTILES), 0, 4) < 3).astype(jnp.int32), jax.random.fold_in(part_splits[3], 1), 0, 1)
    owner_map = jax.random.permutation(streams_of[4], VTILES).astype(jnp.int32)
    return dict(amplitudes=amplitudes, t_mask=t_mask, integrals=integrals, w_mask=w_mask, owner_map=owner_map)


def reference(amplitudes, t_mask, integrals, w_mask, owner_map):
    pair_count = I_OCC * K_OCC
    t_scale = t_mask.astype(jnp.bfloat16)
    masked_t = (amplitudes.reshape(pair_count, VTILES, TILE, VTILES, TILE) * t_scale[:, :, None, :, None]).reshape(I_OCC, K_OCC, VIRT, VIRT)
    w_scale = w_mask.astype(jnp.bfloat16)
    masked_w = (integrals.reshape(K_OCC, VTILES, TILE, VTILES, TILE) * w_scale[:, :, None, :, None]).reshape(K_OCC, VIRT, VIRT)
    c_block = VIRT // N_NARROW

    def one_orbital(block):
        total = jnp.zeros((VIRT, VIRT), jnp.float32)
        for index in range(N_NARROW):
            left = block[:, :, index * c_block:(index + 1) * c_block].astype(jnp.float32)
            right = masked_w[:, index * c_block:(index + 1) * c_block, :].astype(jnp.float32)
            term = jnp.einsum("kac,kcb->ab", left, right)
            rounded = lax.optimization_barrier(term.astype(jnp.bfloat16))
            total = total + rounded.astype(jnp.float32)
        return total.astype(jnp.bfloat16)

    cycle = lax.map(one_orbital, masked_t)
    return cycle.reshape(I_OCC, VTILES, TILE, VIRT)[:, owner_map].reshape(I_OCC, VIRT, VIRT)
```

```python
import jax
import jax.numpy as jnp
from jax import lax
from jax.experimental import pallas as pl
from jax.experimental.pallas import tpu as pltpu
from jax.sharding import PartitionSpec as P

BF16 = jnp.bfloat16
F32 = jnp.float32

SUM_HOME = [(0, 2), (0, 3), (1, 2)]
SUM_AWAY = [(1, 3), (2, 2), (2, 3)]
SUM_LAST = [(3, 2), (3, 3)]
NEAR = [(0, 1), (1, 1), (2, 1), (3, 1)]
OWN = [(0, 0), (1, 0), (2, 0), (3, 0)]


def add(left, right):
    return (left.astype(F32) + right.astype(F32)).astype(BF16)


def order_tiles(meta, owner_map, amps, t_scale, tile_size):
    block_count = meta.shape[1]
    pair_count, virt_count, c_here = amps.shape
    tile_count = owner_map.shape[0]
    tiles = tile_count // 4
    k_count = 2

    def tile_of(j, g, meta, owner):
        return owner[meta[1, g] * tiles + j]

    def kernel(meta, owner, scale_ref, *refs):
        out_ref = refs[-1]
        g = pl.program_id(0)
        for j in range(tiles):
            tile = tile_of(j, g, meta, owner)
            for k in range(k_count):
                scale = scale_ref[meta[0, g] * k_count + k, pl.ds(tile, 1), :]
                part = refs[j][k].astype(F32) * scale
                out_ref[0, k, pl.ds(j * tile_size, tile_size), :] = part.astype(BF16)

    in_specs = [pl.BlockSpec(t_scale.shape, lambda g, meta, owner: (0, 0, 0))]
    for j in range(tiles):
        in_specs.append(
            pl.BlockSpec(
                (k_count, tile_size, c_here),
                lambda g, meta, owner, j=j: (meta[0, g], tile_of(j, g, meta, owner), 0),
            )
        )
    rows = tiles * tile_size
    return pl.pallas_call(
        kernel,
        out_shape=jax.ShapeDtypeStruct((block_count, k_count, rows, c_here), BF16),
        grid_spec=pltpu.PrefetchScalarGridSpec(
            num_scalar_prefetch=2,
            grid=(block_count,),
            in_specs=in_specs,
            out_specs=pl.BlockSpec(
                (1, k_count, rows, c_here), lambda g, meta, owner: (g, 0, 0, 0)
            ),
        ),
        compiler_params=pltpu.CompilerParams(vmem_limit_bytes=32 * 2**20),
        cost_estimate=pl.CostEstimate(
            flops=0, bytes_accessed=4 * block_count * k_count * rows * c_here, transcendentals=0
        ),
        name="order_tiles",
    )(meta, owner_map, t_scale, *([amps] * tiles))


def mask_integrals(core, integrals, w_scale, tile_size):
    k_count, c_rows, b_cols = integrals.shape
    half = c_rows // 2
    tiles = half // tile_size

    def kernel(core, scale_ref, in_ref, out_ref):
        for j in range(tiles):
            rows = pl.ds(j * tile_size, tile_size)
            scale = scale_ref[0, 0, pl.ds(j, 1), :]
            out_ref[0, 0, rows, :] = (in_ref[0, 0, rows, :].astype(F32) * scale).astype(BF16)

    return pl.pallas_call(
        kernel,
        out_shape=jax.ShapeDtypeStruct((k_count, 2, half, b_cols), BF16),
        grid_spec=pltpu.PrefetchScalarGridSpec(
            num_scalar_prefetch=1,
            grid=(k_count, 2),
            in_specs=[
                pl.BlockSpec((1, 1, tiles, b_cols), lambda k, h, core: (k, (h + core[0]) % 2, 0, 0)),
                pl.BlockSpec((1, 1, half, b_cols), lambda k, h, core: (k, (h + core[0]) % 2, 0, 0)),
            ],
            out_specs=pl.BlockSpec((1, 1, half, b_cols), lambda k, h, core: (k, h, 0, 0)),
        ),
        compiler_params=pltpu.CompilerParams(vmem_limit_bytes=32 * 2**20),
        name="mask_integrals",
    )(
        core,
        w_scale.reshape(k_count, 2, tiles, b_cols),
        integrals.reshape(k_count, 2, half, b_cols),
    )


def contract(mine, theirs, weights, index):
    _, k_count, rows, half = mine.shape
    b_cols = weights.shape[3]
    steps = 2

    def kernel(mine_ref, theirs_ref, weights_ref, out_ref):
        total = None
        for k in range(k_count):
            for h, ref in enumerate((mine_ref, theirs_ref)):
                term = jnp.dot(ref[0, k], weights_ref[k, h], preferred_element_type=F32)
                total = term if total is None else total + term
        out_ref[...] = total.astype(BF16)

    block = pl.BlockSpec((1, k_count, rows // steps, half), lambda r: (index, 0, r, 0))
    return pl.pallas_call(
        kernel,
        out_shape=jax.ShapeDtypeStruct((rows, b_cols), BF16),
        grid=(steps,),
        in_specs=[block, block, pl.BlockSpec(weights.shape, lambda r: (0, 0, 0, 0))],
        out_specs=pl.BlockSpec((rows // steps, b_cols), lambda r: (r, 0)),
        compiler_params=pltpu.CompilerParams(vmem_limit_bytes=40 * 2**20),
        cost_estimate=pl.CostEstimate(
            flops=4 * k_count * rows * half * b_cols,
            bytes_accessed=2 * (weights.size + 2 * k_count * rows * half + rows * b_cols),
            transcendentals=0,
        ),
        name="contract",
    )(mine, theirs, weights)


def plane_shards(amplitudes, t_mask, integrals, w_mask, owner_map):
    tile_size = integrals.shape[1] // w_mask.shape[1]
    at_wide = lax.axis_index("wide")
    home = lax.axis_index("narrow") == at_wide // 2
    core = lax.axis_index("sub")
    both = ("wide", "narrow")

    def device(w, at_home):
        return w * 2 + (w // 2 if at_home else 1 - w // 2)

    def move(x, pairs):
        return lax.ppermute(x, both, pairs)

    inward = [(device(w, False), device(w, True)) for w in range(4)]
    outward = [(device(w, True), device(w, False)) for w in range(4)]

    def along(home_distance, away_distance):
        pairs = []
        for w in range(4):
            if home_distance is not None:
                pairs.append((device(w, True), device(w, True) % 2 + 2 * (w ^ home_distance)))
            if away_distance is not None:
                pairs.append((device(w, False), device(w, False) % 2 + 2 * (w ^ away_distance)))
        return pairs

    t_scale = jnp.repeat(t_mask.astype(F32), tile_size, axis=2)
    w_scale = jnp.repeat(w_mask.astype(F32), tile_size, axis=2)
    weights = mask_integrals(core.reshape(1), integrals, w_scale, tile_size)

    def partial_sums(home_blocks, away_blocks):
        home_meta = jnp.array(home_blocks, jnp.int32).T
        away_meta = jnp.array(away_blocks, jnp.int32).T
        meta = jnp.where(home, home_meta, away_meta)
        meta = jnp.stack([meta[0], meta[1] ^ at_wide])
        mine = order_tiles(meta, owner_map, amplitudes, t_scale, tile_size)
        theirs = lax.ppermute(mine, "sub", [(0, 1), (1, 0)])
        return [contract(mine, theirs, weights, g) for g in range(len(home_blocks))]

    give, keep, last = [], [], []
    give_0, last_0 = partial_sums([SUM_AWAY[0], SUM_LAST[0]], [SUM_HOME[0], SUM_LAST[0]])
    keep_0, give_1, keep_1 = partial_sums(
        [SUM_HOME[0], SUM_AWAY[1], SUM_HOME[1]], [SUM_AWAY[0], SUM_HOME[1], SUM_AWAY[1]]
    )
    last_1, give_2, keep_2 = partial_sums(
        [SUM_LAST[1], SUM_AWAY[2], SUM_HOME[2]], [SUM_LAST[1], SUM_HOME[2], SUM_AWAY[2]]
    )
    near = partial_sums(NEAR, NEAR)
    own = partial_sums(OWN, OWN)

    rows, b_cols = own[0].shape
    out = jnp.zeros((8, rows, b_cols), BF16)

    def place(out, value, home_block, away_block):
        def slot(block):
            return ((at_wide ^ block[1]) % 2) * 4 + block[0]

        where = jnp.where(home, slot(home_block), slot(away_block))
        return lax.dynamic_update_slice(out, value[None], (where, 0, 0))

    last_far = []
    for block, value in zip(SUM_LAST, (last_0, last_1)):
        arrived = move(value, along(block[1], block[1]))
        last_far.append((arrived, move(arrived, outward)))
    far = []
    for index, (given, kept) in enumerate(zip((give_0, give_1, give_2), (keep_0, keep_1, keep_2))):
        total = add(kept, move(given, inward + outward))
        arrived = move(total, along(SUM_HOME[index][1], SUM_AWAY[index][1]))
        far.append((arrived, move(arrived, outward)))
    near_far = []
    for value in near:
        total = add(value, move(value, inward))
        near_far.append(move(total, along(1, None)))
    own_sums = [add(value, move(value, inward)) for value in own]

    out = place(out, jnp.where(home, near_far[0], far[0][0]), NEAR[0], SUM_HOME[0])
    out = place(out, jnp.where(home, near_far[1], far[1][0]), NEAR[1], SUM_HOME[1])
    out = place(out, jnp.where(home, near_far[2], far[2][0]), NEAR[2], SUM_HOME[2])
    out = place(out, jnp.where(home, near_far[3], far[0][1]), NEAR[3], SUM_AWAY[0])
    out = place(out, jnp.where(home, own_sums[0], far[1][1]), OWN[0], SUM_AWAY[1])
    out = place(out, jnp.where(home, own_sums[1], far[2][1]), OWN[1], SUM_AWAY[2])
    out = place(out, jnp.where(home, own_sums[2], add(*last_far[0])), OWN[2], SUM_LAST[0])
    out = place(out, jnp.where(home, own_sums[3], add(*last_far[1])), OWN[3], SUM_LAST[1])
    return out


def regroup_rows(amps, owner_map, tile_size):
    pair_count, virt_count, c_count = amps.shape
    ordered = jnp.take(
        amps.reshape(pair_count, virt_count // tile_size, tile_size, c_count), owner_map, axis=1
    )
    ordered = ordered.reshape(pair_count, virt_count, c_count)
    return lax.all_to_all(ordered, "wide", split_axis=1, concat_axis=0, tiled=True)


def join_halves(amps):
    return lax.all_gather(amps, "sub", axis=2, tiled=True)


def shards(amplitudes, t_mask, integrals, w_mask, owner_map):
    tile_count = owner_map.shape[0]
    pair_here, virt_count, c_here = amplitudes.shape
    tile_size = virt_count // tile_count
    t_scale = t_mask.astype(jnp.bfloat16)
    masked_t = (
        amplitudes.reshape(pair_here, tile_count, tile_size, t_mask.shape[2], tile_size)
        * t_scale[:, :, None, :, None]
    )
    masked_t = masked_t.reshape(pair_here, virt_count, c_here)
    k_count, c_rows, b_cols = integrals.shape
    w_scale = w_mask.astype(jnp.bfloat16)
    masked_w = (
        integrals.reshape(k_count, w_mask.shape[1], tile_size, w_mask.shape[2], tile_size)
        * w_scale[:, :, None, :, None]
    )
    masked_w = masked_w.reshape(k_count, c_rows, b_cols)
    regrouped = join_halves(regroup_rows(masked_t, owner_map, tile_size))
    pair_count, row_count, col_count = regrouped.shape
    occ_count = pair_count // k_count
    blocks = regrouped.reshape(occ_count, k_count, row_count, col_count)
    partial_value = jnp.einsum(
        "ikac,kcb->iab", blocks, masked_w, preferred_element_type=jnp.float32
    )
    rounded = partial_value.astype(jnp.bfloat16)
    return (
        lax.psum_scatter(rounded, "narrow", scatter_dimension=0, tiled=True)
        .astype(jnp.float32)
        .astype(jnp.bfloat16)
    )


def solution(mesh):
    in_specs = (
        P(("group", "wide"), None, ("narrow", "sub")),
        P(("group", "wide"), None, ("narrow", "sub")),
        P("group", "narrow", "sub"),
        P("group", "narrow", "sub"),
        P(),
    )
    out_specs = P(("group", "narrow"), "wide", "sub")
    planes = (mesh.shape["wide"], mesh.shape["narrow"], mesh.shape["sub"]) == (4, 2, 2)
    body = plane_shards if planes else shards
    return jax.shard_map(body, mesh=mesh, in_specs=in_specs, out_specs=out_specs, check_vma=False)
```

```python
import jax
import jax.numpy as jnp
from jax import lax
from jax.experimental import pallas as pl
from jax.experimental.pallas import tpu as pltpu
from jax.sharding import PartitionSpec as P

BF16 = jnp.bfloat16
F32 = jnp.float32
MIB = 2**20

SUM_HOME = [(0, 2), (1, 3), (2, 2)]
SUM_AWAY = [(0, 3), (1, 2), (2, 3), (3, 2)]
SUM_LAST = [(3, 3)]
NEAR = [(0, 1), (1, 1), (2, 1), (3, 1)]
OWN = [(0, 0), (1, 0), (2, 0), (3, 0)]
HOME_SLOTS = [
    SUM_LAST[0], SUM_AWAY[0], SUM_AWAY[1], SUM_HOME[0], SUM_AWAY[2], SUM_HOME[1], SUM_HOME[2], SUM_AWAY[3], *NEAR, *OWN
]
AWAY_SLOTS = [
    SUM_LAST[0], SUM_HOME[0], SUM_HOME[1], SUM_AWAY[0], SUM_HOME[2], SUM_AWAY[1], SUM_AWAY[2], SUM_AWAY[3], *NEAR, *OWN
]

ANY = pl.BlockSpec(memory_space=pl.ANY)


COST = pl.CostEstimate(flops=10**12, bytes_accessed=10**9, transcendentals=0)


class Chain:
    def __init__(self, first):
        self.before = first

    def call(self, kernel, name, operands, out_shape, grid, in_specs, out_specs, prefetch=(), aliases=None):
        skip = len(prefetch) + len(operands)

        def body(*refs):
            kernel(*refs[:skip], *refs[skip + 1:])

        result = pl.pallas_call(
            body,
            out_shape=out_shape,
            grid_spec=pltpu.PrefetchScalarGridSpec(
                num_scalar_prefetch=len(prefetch),
                grid=grid,
                in_specs=[*in_specs, ANY],
                out_specs=out_specs,
            ),
            input_output_aliases=aliases or {},
            compiler_params=pltpu.CompilerParams(vmem_limit_bytes=64 * MIB),
            cost_estimate=COST,
            name=name,
        )(*prefetch, *operands, self.before)
        self.before = result
        return result

    def order_tiles(self, meta, owner_map, amps, t_scale, tile_size, first, count):
        c_here = amps.shape[2]
        tiles = owner_map.shape[0] // 4
        rows = tiles * tile_size
        k_count = 2

        def tile_of(j, g, meta, owner):
            return owner[meta[1, first + g] * tiles + j]

        def kernel(meta, owner, scale_ref, *refs):
            out_ref = refs[-1]
            g = pl.program_id(0)
            for j in range(tiles):
                tile = tile_of(j, g, meta, owner)
                for k in range(k_count):
                    scale = scale_ref[meta[0, first + g] * k_count + k, pl.ds(tile, 1), :]
                    part = refs[j][k].astype(F32) * scale
                    out_ref[0, k, pl.ds(j * tile_size, tile_size), :] = part.astype(BF16)

        in_specs = [pl.BlockSpec(t_scale.shape, lambda g, meta, owner: (0, 0, 0))]
        for j in range(tiles):
            in_specs.append(
                pl.BlockSpec(
                    (k_count, tile_size, c_here),
                    lambda g, meta, owner, j=j: (meta[0, first + g], tile_of(j, g, meta, owner), 0),
                )
            )
        return self.call(
            kernel,
            "order_tiles",
            (t_scale, *([amps] * tiles)),
            jax.ShapeDtypeStruct((count, k_count, rows, c_here), BF16),
            (count,),
            in_specs,
            pl.BlockSpec((1, k_count, rows, c_here), lambda g, meta, owner: (g, 0, 0, 0)),
            prefetch=(meta, owner_map),
        )

    def mask_integrals(self, core, integrals, w_scale, tile_size):
        k_count, c_rows, b_cols = integrals.shape
        half = c_rows // 2
        tiles = half // tile_size

        def kernel(core, scale_ref, in_ref, out_ref):
            for j in range(tiles):
                rows = pl.ds(j * tile_size, tile_size)
                scale = scale_ref[0, 0, pl.ds(j, 1), :]
                out_ref[0, 0, rows, :] = (in_ref[0, 0, rows, :].astype(F32) * scale).astype(BF16)

        def source(k, h, core):
            return (k, (h + core[0]) % 2, 0, 0)

        return self.call(
            kernel,
            "mask_integrals",
            (
                w_scale.reshape(k_count, 2, tiles, b_cols),
                integrals.reshape(k_count, 2, half, b_cols),
            ),
            jax.ShapeDtypeStruct((k_count, 2, half, b_cols), BF16),
            (k_count, 2),
            [
                pl.BlockSpec((1, 1, tiles, b_cols), source),
                pl.BlockSpec((1, 1, half, b_cols), source),
            ],
            pl.BlockSpec((1, 1, half, b_cols), lambda k, h, core: (k, h, 0, 0)),
            prefetch=(core,),
        )

    def contract(self, tiles, weights, first, count=1):
        mine, theirs = tiles
        _, k_count, rows, half = mine.shape
        b_cols = weights.shape[3]
        steps = 2

        def kernel(mine_ref, theirs_ref, weights_ref, out_ref):
            total = None
            for k in range(k_count):
                for h, ref in enumerate((mine_ref, theirs_ref)):
                    term = jnp.dot(ref[0, k], weights_ref[k, h], preferred_element_type=F32)
                    total = term if total is None else total + term
            out_ref[0] = total.astype(BF16)

        block = pl.BlockSpec((1, k_count, rows // steps, half), lambda g, r: (first + g, 0, r, 0))
        return self.call(
            kernel,
            "contract",
            (mine, theirs, weights),
            jax.ShapeDtypeStruct((count, rows, b_cols), BF16),
            (count, steps),
            [block, block, pl.BlockSpec(weights.shape, lambda g, r: (0, 0, 0, 0))],
            pl.BlockSpec((1, rows // steps, b_cols), lambda g, r: (g, r, 0)),
        )

    def add(self, left, right):
        count, rows, b_cols = left.shape
        steps = 2

        def kernel(left_ref, right_ref, out_ref):
            out_ref[...] = (left_ref[...].astype(F32) + right_ref[...].astype(F32)).astype(BF16)

        block = pl.BlockSpec((1, rows // steps, b_cols), lambda g, r: (g, r, 0))
        return self.call(
            kernel,
            "add",
            (left, right),
            jax.ShapeDtypeStruct(left.shape, BF16),
            (count, steps),
            [block, block],
            block,
        )

    def hand_on(self, value):
        return self.call(
            lambda *refs: None,
            "hand_on",
            (value,),
            jax.ShapeDtypeStruct(value.shape, value.dtype),
            (1,),
            [ANY],
            ANY,
            aliases={0: 0},
        )

    def place(self, out, where, home_terms, away_terms):
        terms = (*home_terms, *away_terms)
        _, rows, b_cols = terms[0][0].shape
        steps = 2
        block_count = 8

        def total(refs):
            if len(refs) == 1:
                return refs[0][...]
            return (refs[0][...].astype(F32) + refs[1][...].astype(F32)).astype(BF16)

        def kernel(where, *refs):
            out_ref = refs[-1]
            split = len(home_terms)

            @pl.when(where[0] == 1)
            def _():
                out_ref[...] = total(refs[:split])

            @pl.when(where[0] == 0)
            def _():
                out_ref[...] = total(refs[split:len(terms)])

        def block(index):
            return pl.BlockSpec((1, rows // steps, b_cols), lambda r, where: (index, r, 0))

        held = () if out is None else (out,)
        return self.call(
            kernel,
            "place",
            (*[array for array, _ in terms], *held),
            jax.ShapeDtypeStruct((block_count, rows, b_cols), BF16),
            (steps,),
            [block(index) for _, index in terms] + [ANY] * len(held),
            pl.BlockSpec((1, rows // steps, b_cols), lambda r, where: (where[1], r, 0)),
            prefetch=(where,),
            aliases={1 + len(terms): 0} if held else None,
        )


def plane_shards(amplitudes, t_mask, integrals, w_mask, owner_map):
    tile_size = integrals.shape[1] // w_mask.shape[1]
    at_wide = lax.axis_index("wide")
    home = lax.axis_index("narrow") == at_wide // 2
    core = lax.axis_index("sub").reshape(1)
    both = ("wide", "narrow")

    def device(w, at_home):
        return w * 2 + (w // 2 if at_home else 1 - w // 2)

    def move(x, pairs):
        return lax.ppermute(x, both, pairs)

    inward = [(device(w, False), device(w, True)) for w in range(4)]
    outward = [(device(w, True), device(w, False)) for w in range(4)]

    def along(home_distance, away_distance):
        pairs = []
        for w in range(4):
            for at_home, distance in ((True, home_distance), (False, away_distance)):
                if distance is not None:
                    here = device(w, at_home)
                    pairs.append((here, here % 2 + 2 * (w ^ distance)))
        return pairs

    home_meta = jnp.array(HOME_SLOTS, jnp.int32).T
    away_meta = jnp.array(AWAY_SLOTS, jnp.int32).T
    meta = jnp.where(home, home_meta, away_meta)
    meta = jnp.stack([meta[0], meta[1] ^ at_wide])
    t_scale = jnp.repeat(t_mask.astype(F32), tile_size, axis=2)
    w_scale = jnp.repeat(w_mask.astype(F32), tile_size, axis=2)

    chain = Chain(meta)

    def ordered(first, count):
        mine = chain.order_tiles(meta, owner_map, amplitudes, t_scale, tile_size, first, count)
        return mine, lax.ppermute(mine, "sub", [(0, 1), (1, 0)])

    def where(home_block, away_block):
        def slot(block):
            return ((at_wide ^ block[1]) % 2) * 4 + block[0]

        return jnp.stack([home.astype(jnp.int32), jnp.where(home, slot(home_block), slot(away_block))])

    swap = inward + outward

    def contract(tiles, first, count=1):
        return chain.contract(tiles, weights, first, count)

    tiles_last = ordered(0, 1)
    tiles_first = ordered(1, 1)
    weights = chain.mask_integrals(core, integrals, w_scale, tile_size)
    tiles_a = ordered(2, 3)
    last_far = move(contract(tiles_last, 0), along(SUM_LAST[0][1], SUM_LAST[0][1]))
    given_0 = move(contract(tiles_first, 0), swap)
    given_1 = move(contract(tiles_a, 0), swap)
    tiles_b = ordered(5, 3)
    kept_0 = contract(tiles_a, 1)
    kept_1 = contract(tiles_b, 0)
    tiles_c = ordered(8, 8)
    far_0 = move(chain.add(kept_0, given_0), along(SUM_HOME[0][1], SUM_AWAY[0][1]))
    given_2 = move(contract(tiles_a, 2), swap)
    kept_2 = contract(tiles_b, 1)
    far_1 = move(chain.add(kept_1, given_1), along(SUM_HOME[1][1], SUM_AWAY[1][1]))
    last_far = chain.hand_on(last_far)
    near_a = contract(tiles_c, 0, 2)
    near_a_in = move(near_a, inward)
    extra = contract(tiles_b, 2)
    extra_out = move(extra, outward)

    total_2 = chain.add(kept_2, given_2)
    last_far = chain.hand_on(last_far)
    last_over = move(last_far, outward)

    total_3 = chain.add(extra, extra_out)
    far_0 = chain.hand_on(far_0)
    far_2 = move(chain.hand_on(total_2), along(SUM_HOME[2][1], SUM_AWAY[2][1]))
    near_b = contract(tiles_c, 2, 2)
    near_b_in = move(near_b, inward)

    last_over = chain.hand_on(last_over)
    far_0 = chain.hand_on(far_0)
    over_0 = move(far_0, outward)
    near_a_far = move(chain.add(near_a, near_a_in), along(1, None))

    over_0 = chain.hand_on(over_0)
    far_1 = chain.hand_on(far_1)
    over_1 = move(far_1, outward)
    own_a = contract(tiles_c, 4, 3)
    own_a_in = move(own_a, inward)

    near_b_far = move(chain.add(near_b, near_b_in), along(1, None))
    over_1 = chain.hand_on(over_1)
    far_3 = move(chain.hand_on(total_3), along(None, SUM_AWAY[3][1]))

    far_2 = chain.hand_on(far_2)
    over_2 = move(far_2, outward)
    out = chain.place(None, where(NEAR[0], SUM_LAST[0]), [(near_a_far, 0)], [(last_far, 0), (last_over, 0)])
    out = chain.place(out, where(NEAR[1], SUM_HOME[0]), [(near_a_far, 1)], [(far_0, 0)])
    own_b = contract(tiles_c, 7)
    own_b_in = move(own_b, inward)

    over_2 = chain.hand_on(over_2)
    far_3 = chain.hand_on(far_3)
    over_3 = move(far_3, outward)
    out = chain.place(out, where(NEAR[2], SUM_HOME[1]), [(near_b_far, 0)], [(far_1, 0)])
    out = chain.place(out, where(NEAR[3], SUM_AWAY[0]), [(near_b_far, 1)], [(over_0, 0)])
    out = chain.place(out, where(OWN[0], SUM_AWAY[1]), [(own_a, 0), (own_a_in, 0)], [(over_1, 0)])
    out = chain.place(out, where(OWN[1], SUM_HOME[2]), [(own_a, 1), (own_a_in, 1)], [(far_2, 0)])
    out = chain.place(out, where(OWN[2], SUM_AWAY[2]), [(own_a, 2), (own_a_in, 2)], [(over_2, 0)])
    out = chain.place(out, where(OWN[3], SUM_AWAY[3]), [(own_b, 0), (own_b_in, 0)], [(over_3, 0)])
    return out


def regroup_rows(amps, owner_map, tile_size):
    pair_count, virt_count, c_count = amps.shape
    ordered = jnp.take(
        amps.reshape(pair_count, virt_count // tile_size, tile_size, c_count), owner_map, axis=1
    )
    ordered = ordered.reshape(pair_count, virt_count, c_count)
    return lax.all_to_all(ordered, "wide", split_axis=1, concat_axis=0, tiled=True)


def join_halves(amps):
    return lax.all_gather(amps, "sub", axis=2, tiled=True)


def shards(amplitudes, t_mask, integrals, w_mask, owner_map):
    tile_count = owner_map.shape[0]
    pair_here, virt_count, c_here = amplitudes.shape
    tile_size = virt_count // tile_count
    t_scale = t_mask.astype(jnp.bfloat16)
    masked_t = (
        amplitudes.reshape(pair_here, tile_count, tile_size, t_mask.shape[2], tile_size)
        * t_scale[:, :, None, :, None]
    )
    masked_t = masked_t.reshape(pair_here, virt_count, c_here)
    k_count, c_rows, b_cols = integrals.shape
    w_scale = w_mask.astype(jnp.bfloat16)
    masked_w = (
        integrals.reshape(k_count, w_mask.shape[1], tile_size, w_mask.shape[2], tile_size)
        * w_scale[:, :, None, :, None]
    )
    masked_w = masked_w.reshape(k_count, c_rows, b_cols)
    regrouped = join_halves(regroup_rows(masked_t, owner_map, tile_size))
    pair_count, row_count, col_count = regrouped.shape
    occ_count = pair_count // k_count
    blocks = regrouped.reshape(occ_count, k_count, row_count, col_count)
    partial_value = jnp.einsum(
        "ikac,kcb->iab", blocks, masked_w, preferred_element_type=jnp.float32
    )
    rounded = partial_value.astype(jnp.bfloat16)
    return (
        lax.psum_scatter(rounded, "narrow", scatter_dimension=0, tiled=True)
        .astype(jnp.float32)
        .astype(jnp.bfloat16)
    )


def solution(mesh):
    in_specs = (
        P(("group", "wide"), None, ("narrow", "sub")),
        P(("group", "wide"), None, ("narrow", "sub")),
        P("group", "narrow", "sub"),
        P("group", "narrow", "sub"),
        P(),
    )
    out_specs = P(("group", "narrow"), "wide", "sub")
    planes = (mesh.shape["wide"], mesh.shape["narrow"], mesh.shape["sub"]) == (4, 2, 2)
    body = plane_shards if planes else shards
    return jax.shard_map(body, mesh=mesh, in_specs=in_specs, out_specs=out_specs, check_vma=False)
```

```python
import jax
import jax.numpy as jnp
from jax import lax
from jax.experimental import pallas as pl
from jax.experimental.pallas import tpu as pltpu
from jax.sharding import PartitionSpec as P

BF16 = jnp.bfloat16
F32 = jnp.float32
MIB = 2**20

SUM_HOME = [(0, 2), (1, 3), (2, 2)]
SUM_AWAY = [(0, 3), (1, 2), (2, 3), (3, 2)]
SUM_LAST = (3, 3)
NEAR = [(0, 1), (1, 1), (2, 1), (3, 1)]
OWN = [(0, 0), (1, 0), (2, 0), (3, 0)]

ANY = pl.BlockSpec(memory_space=pl.ANY)
COST = pl.CostEstimate(flops=10**12, bytes_accessed=10**9, transcendentals=0)


def pick(values, index):
    chosen = values[0]
    for at, value in enumerate(values[1:], 1):
        chosen = jnp.where(index == at, value, chosen)
    return chosen


def widen(mask, tile_size, tile_dim):
    tiles = mask.shape[tile_dim]
    shape = (tiles, tiles * tile_size)
    column = lax.broadcasted_iota(jnp.int32, shape, 1)
    first = lax.broadcasted_iota(jnp.int32, shape, 0) * tile_size
    spread = (column >= first) & (column < first + tile_size)
    return lax.dot_general(
        mask.astype(F32), spread.astype(F32), (((tile_dim,), (0,)), ((), ())), preferred_element_type=F32
    )


class Chain:
    def __init__(self):
        self.before = None

    def call(
        self, kernel, name, operands, out_shape, grid, in_specs, out_specs, prefetch=(), aliases=None, scratch=()
    ):
        skip = len(prefetch) + len(operands)
        before = self.before
        known = before is None or any(before is operand for operand in operands)
        after = () if known else (before,)

        def body(*refs):
            kernel(*refs[:skip], *refs[skip + len(after):])

        result = pl.pallas_call(
            body,
            out_shape=out_shape,
            grid_spec=pltpu.PrefetchScalarGridSpec(
                num_scalar_prefetch=len(prefetch),
                grid=grid,
                in_specs=[*in_specs, *[ANY] * len(after)],
                out_specs=out_specs,
                scratch_shapes=scratch,
            ),
            input_output_aliases=aliases or {},
            compiler_params=pltpu.CompilerParams(vmem_limit_bytes=64 * MIB),
            cost_estimate=COST,
            name=name,
        )(*prefetch, *operands, *after)
        self.before = result[0] if isinstance(result, (list, tuple)) else result
        return result

    def order_tiles(self, role, owner_map, amps, t_mask, tile_size, blocks):
        c_here = amps.shape[2]
        tiles = owner_map.shape[0] // 4
        rows = tiles * tile_size
        k_count = 2

        def choose(role, g, part):
            home, away = ([pair[at][part] for pair in blocks] for at in (0, 1))
            return pick([h if h == a else jnp.where(role[0] == 1, h, a) for h, a in zip(home, away)], g)

        def tile_of(j, g, role, owner):
            return owner[(role[1] ^ choose(role, g, 1)) * tiles + j]

        def kernel(role, owner, mask_ref, *refs):
            out_ref, wide_ref = refs[-2:]
            g = pl.program_id(0)
            for k in range(k_count):
                wide_ref[k] = widen(mask_ref[k], tile_size, 0)
            for j in range(tiles):
                tile = tile_of(j, g, role, owner)
                for k in range(k_count):
                    scale = wide_ref[k, pl.ds(tile, 1), :].astype(BF16)
                    out_ref[0, pl.ds(j * tile_size, tile_size), pl.ds(k * c_here, c_here)] = refs[j][k] * scale

        def pair(g, role, owner):
            return (choose(role, g, 0), 0, 0)

        in_specs = [pl.BlockSpec((k_count, *t_mask.shape[1:]), pair)]
        for j in range(tiles):
            in_specs.append(
                pl.BlockSpec(
                    (k_count, tile_size, c_here),
                    lambda g, role, owner, j=j: (choose(role, g, 0), tile_of(j, g, role, owner), 0),
                )
            )
        return self.call(
            kernel,
            "order_tiles",
            (t_mask, *([amps] * tiles)),
            jax.ShapeDtypeStruct((len(blocks), rows, k_count * c_here), BF16),
            (len(blocks),),
            in_specs,
            pl.BlockSpec((1, rows, k_count * c_here), lambda g, role, owner: (g, 0, 0)),
            prefetch=(role, owner_map),
            scratch=[pltpu.VMEM((k_count, t_mask.shape[2], c_here), F32)],
        )

    def contract_first(self, role, tiles, integrals, w_mask, tile_size):
        mine, theirs = tiles
        k_count, c_rows, b_cols = integrals.shape
        count, rows, _ = mine.shape
        half = c_rows // 2
        half_tiles = half // tile_size

        def kernel(role, mask_ref, in_ref, mine_ref, theirs_ref, *refs):
            *out_refs, weights_ref, wide_ref, total_ref = refs
            h, k = pl.program_id(0), pl.program_id(1)
            wide_ref[...] = widen(mask_ref[0], tile_size, 1)
            for j in range(half_tiles):
                at = pl.ds(j * tile_size, tile_size)
                scale = wide_ref[pl.ds((h ^ role[2]) * half_tiles + j, 1), :].astype(BF16)
                weights_ref[0, at, :] = in_ref[0, at, :] * scale

            def term(ref, block):
                return jnp.dot(ref[block], weights_ref[0], preferred_element_type=F32)

            for block in range(count):

                @pl.when((h == 0) & (k == 0))
                def _(block=block):
                    total_ref[block] = term(mine_ref, block)

                @pl.when((h == 0) & (k > 0))
                def _(block=block):
                    total_ref[block] += term(mine_ref, block)

                @pl.when((h == 1) & (k < k_count - 1))
                def _(block=block):
                    total_ref[block] += term(theirs_ref, block)

                @pl.when((h == 1) & (k == k_count - 1))
                def _(block=block):
                    out_refs[block][0] = (total_ref[block] + term(theirs_ref, block)).astype(BF16)

        block = pl.BlockSpec((count, rows, half), lambda h, k, role: (0, 0, k))
        return self.call(
            kernel,
            "contract_first",
            (w_mask, integrals, mine, theirs),
            [
                *[jax.ShapeDtypeStruct((1, rows, b_cols), BF16)] * count,
                jax.ShapeDtypeStruct((2, k_count * half, b_cols), BF16),
            ],
            (2, k_count),
            [
                pl.BlockSpec((1, *w_mask.shape[1:]), lambda h, k, role: (k, 0, 0)),
                pl.BlockSpec((1, half, b_cols), lambda h, k, role: (k, h ^ role[2], 0)),
                block,
                block,
            ],
            [
                *[pl.BlockSpec((1, rows, b_cols), lambda h, k, role: (0, 0, 0))] * count,
                pl.BlockSpec((1, half, b_cols), lambda h, k, role: (h, k, 0)),
            ],
            prefetch=(role,),
            scratch=[pltpu.VMEM((w_mask.shape[1], b_cols), F32), pltpu.VMEM((count, rows, b_cols), F32)],
        )

    def contract_apart(self, tiles, weights, first, count):
        mine, theirs = tiles
        _, rows, depth = mine.shape
        b_cols = weights.shape[2]
        steps = 2

        def kernel(mine_ref, theirs_ref, weights_ref, *out_refs):
            g = pl.program_id(0)
            total = jnp.dot(mine_ref[0], weights_ref[0], preferred_element_type=F32)
            total += jnp.dot(theirs_ref[0], weights_ref[1], preferred_element_type=F32)
            for at in range(count):

                @pl.when(g == at)
                def _(out_ref=out_refs[at]):
                    out_ref[0] = total.astype(BF16)

        block = pl.BlockSpec((1, rows // steps, depth), lambda g, r: (first + g, r, 0))

        def out_block(at):
            return pl.BlockSpec(
                (1, rows // steps, b_cols),
                lambda g, r: (0, jnp.where(g < at, 0, jnp.where(g > at, steps - 1, r)), 0),
            )

        return self.call(
            kernel,
            "contract_apart",
            (mine, theirs, weights),
            [jax.ShapeDtypeStruct((1, rows, b_cols), BF16)] * count,
            (count, steps),
            [block, block, pl.BlockSpec(weights.shape, lambda g, r: (0, 0, 0))],
            [out_block(at) for at in range(count)],
        )

    def contract(self, role, tiles, weights, first, count=1):
        mine, theirs = tiles
        _, rows, depth = mine.shape
        b_cols = weights.shape[2]
        steps = 2

        def kernel(role, mine_ref, theirs_ref, weights_ref, out_ref):
            total = jnp.dot(mine_ref[0], weights_ref[0], preferred_element_type=F32)
            total += jnp.dot(theirs_ref[0], weights_ref[1], preferred_element_type=F32)
            out_ref[0] = total.astype(BF16)

        block = pl.BlockSpec((1, rows // steps, depth), lambda g, r, role: (first + g, r, 0))
        return self.call(
            kernel,
            "contract",
            (mine, theirs, weights),
            jax.ShapeDtypeStruct((count, rows, b_cols), BF16),
            (count, steps),
            [block, block, pl.BlockSpec(weights.shape, lambda g, r, role: (0, 0, 0))],
            pl.BlockSpec((1, rows // steps, b_cols), lambda g, r, role: (g, r, 0)),
            prefetch=(role,),
        )

    def add(self, sums):
        steps = 2
        count = len(sums)
        _, rows, b_cols = sums[0][0][0].shape

        def kernel(*refs):
            out_ref = refs[-1]
            g = pl.program_id(0)
            for at in range(count):

                @pl.when(g == at)
                def _(left=refs[2 * at], right=refs[2 * at + 1]):
                    out_ref[...] = (left[...].astype(F32) + right[...].astype(F32)).astype(BF16)

        def block(at, index):
            return pl.BlockSpec(
                (1, rows // steps, b_cols),
                lambda g, r: (index, jnp.where(g < at, 0, jnp.where(g > at, steps - 1, r)), 0),
            )

        return self.call(
            kernel,
            "add",
            tuple(array for both in sums for array, _ in both),
            jax.ShapeDtypeStruct((count, rows, b_cols), BF16),
            (count, steps),
            [block(at, index) for at, both in enumerate(sums) for _, index in both],
            pl.BlockSpec((1, rows // steps, b_cols), lambda g, r: (g, r, 0)),
        )

    def hand_on(self, value):
        return self.call(
            lambda *refs: None,
            "hand_on",
            (value,),
            jax.ShapeDtypeStruct(value.shape, value.dtype),
            (1,),
            [ANY],
            ANY,
            aliases={0: 0},
        )

    def place(self, role, out, home_terms, away_terms, blocks=None, block_count=8):
        terms = (*home_terms, *away_terms)
        _, rows, b_cols = terms[0][0].shape
        steps = 2
        orbitals = block_count // 2

        def total(refs):
            if len(refs) == 1:
                return refs[0][...]
            return (refs[0][...].astype(F32) + refs[1][...].astype(F32)).astype(BF16)

        def kernel(role, *refs):
            out_ref = refs[-1]
            split = len(home_terms)

            @pl.when(role[0] == 1)
            def _():
                out_ref[...] = total(refs[:split])

            @pl.when(role[0] == 0)
            def _():
                out_ref[...] = total(refs[split:len(terms)])

        def block(index):
            return pl.BlockSpec((1, rows // steps, b_cols), lambda r, role: (index, r, 0))

        def slot(role):
            if blocks is None:
                return 0
            orbital, distance = (jnp.where(role[0] == 1, *pair) for pair in zip(*blocks))
            return ((role[1] ^ distance) % 2) * orbitals + orbital

        held = () if out is None else (out,)
        return self.call(
            kernel,
            "place",
            (*[array for array, _ in terms], *held),
            jax.ShapeDtypeStruct((block_count, rows, b_cols), BF16),
            (steps,),
            [block(index) for _, index in terms] + [ANY] * len(held),
            pl.BlockSpec((1, rows // steps, b_cols), lambda r, role: (slot(role), r, 0)),
            prefetch=(role,),
            aliases={1 + len(terms): 0} if held else None,
        )


def plane_shards(amplitudes, t_mask, integrals, w_mask, owner_map):
    tile_size = integrals.shape[1] // w_mask.shape[1]
    at_wide = lax.axis_index("wide")
    home = (lax.axis_index("narrow") == at_wide // 2).astype(jnp.int32)
    role = jnp.stack([home, at_wide, lax.axis_index("sub")])
    masks = jnp.swapaxes(t_mask, 1, 2)
    both = ("wide", "narrow")

    def device(w, at_home):
        return w * 2 + (w // 2 if at_home else 1 - w // 2)

    def move(x, pairs):
        return lax.ppermute(x, both, pairs)

    inward = [(device(w, False), device(w, True)) for w in range(4)]
    outward = [(device(w, True), device(w, False)) for w in range(4)]

    def far(home_distance=None, away_distance=None):
        pairs = []
        for w in range(4):
            keeper = device(w, True) % 2
            for at_home, distance in ((True, home_distance), (False, away_distance)):
                if distance is not None:
                    pairs.append((device(w, at_home), keeper + 2 * (w ^ distance)))
        return pairs

    near = [(device(w, True), device(w, True) % 2 + 2 * (w ^ 1)) for w in range(4)]
    chain = Chain()

    def ordered(blocks):
        mine = chain.order_tiles(role, owner_map, amplitudes, masks, tile_size, blocks)
        return mine, lax.ppermute(mine, "sub", [(0, 1), (1, 0)])

    def contract(tiles, first, count=1):
        return chain.contract(role, tiles, weights, first, count)

    def add(left, right):
        return chain.add([(left, right)])

    def same(block):
        return (block, block)

    def place(out, home_block, away_block, home_terms, away_terms):
        return chain.place(role, out, home_terms, away_terms, (home_block, away_block))

    swap = inward + outward
    give = [(away, home) for home, away in zip(NEAR, SUM_AWAY)]
    keep = list(zip(NEAR, SUM_AWAY))

    tiles_a = ordered([give[0], same(SUM_LAST)])
    tiles_b = ordered([same(SUM_HOME[0]), keep[0]])
    tiles_c = ordered([give[1], same(SUM_HOME[1]), keep[1], give[2]])
    give_0, last, weights = chain.contract_first(role, tiles_a, integrals, w_mask, tile_size)
    got_0 = move(give_0, swap)
    last_away = move(last, far(None, SUM_LAST[1]))
    home_0, keep_0 = chain.contract_apart(tiles_b, weights, 0, 2)
    home_0_in = move(home_0, inward)
    give_1, home_1 = chain.contract_apart(tiles_c, weights, 0, 2)
    last_home = move(last, far(SUM_LAST[1], None))

    round_0 = move(add((keep_0, 0), (got_0, 0)), near + far(None, SUM_AWAY[0][1]))
    got_1 = move(chain.hand_on(give_1), swap)
    keep_1, give_2 = chain.contract_apart(tiles_c, weights, 2, 2)
    tiles_d = ordered([same(SUM_HOME[2]), keep[2], give[3], keep[3], *[same(block) for block in OWN]])
    far_0 = move(add((home_0, 0), (home_0_in, 0)), far(SUM_HOME[0][1], None))
    home_1 = chain.hand_on(home_1)
    home_1_in = move(home_1, inward)
    last_away = chain.hand_on(last_away)
    last_home = chain.hand_on(last_home)

    round_1 = move(add((keep_1, 0), (got_1, 0)), near + far(None, SUM_AWAY[1][1]))
    got_2 = move(chain.hand_on(give_2), swap)
    home_2, keep_2 = chain.contract_apart(tiles_d, weights, 0, 2)
    round_0 = chain.hand_on(round_0)
    far_0 = chain.hand_on(far_0)
    far_1 = move(add((home_1, 0), (home_1_in, 0)), far(SUM_HOME[1][1], None))
    home_2 = chain.hand_on(home_2)
    home_2_in = move(home_2, inward)
    give_3, keep_3 = chain.contract_apart(tiles_d, weights, 2, 2)

    round_2 = move(add((keep_2, 0), (got_2, 0)), near + far(None, SUM_AWAY[2][1]))
    got_3 = move(chain.hand_on(give_3), swap)
    own_012 = contract(tiles_d, 4, 3)
    own_3 = contract(tiles_d, 7)
    round_1 = chain.hand_on(round_1)
    far_1 = chain.hand_on(far_1)
    far_2 = move(add((home_2, 0), (home_2_in, 0)), far(SUM_HOME[2][1], None))
    own_012 = chain.hand_on(own_012)
    own_012_in = move(own_012, inward)
    out = place(None, NEAR[0], SUM_AWAY[0], [(round_0, 0)], [(round_0, 0)])
    out = place(out, NEAR[1], SUM_AWAY[1], [(round_1, 0)], [(round_1, 0)])

    round_3 = move(add((keep_3, 0), (got_3, 0)), near + far(None, SUM_AWAY[3][1]))
    own_3 = chain.hand_on(own_3)
    own_3_in = move(own_3, inward)
    out = place(out, NEAR[2], SUM_AWAY[2], [(round_2, 0)], [(round_2, 0)])
    far_2 = chain.hand_on(far_2)
    out = place(out, OWN[0], SUM_LAST, [(own_012, 0), (own_012_in, 0)], [(last_away, 0), (last_home, 0)])
    out = place(out, OWN[1], SUM_HOME[0], [(own_012, 1), (own_012_in, 1)], [(far_0, 0)])
    out = place(out, OWN[2], SUM_HOME[1], [(own_012, 2), (own_012_in, 2)], [(far_1, 0)])
    out = place(out, NEAR[3], SUM_AWAY[3], [(round_3, 0)], [(round_3, 0)])
    out = place(out, OWN[3], SUM_HOME[2], [(own_3, 0), (own_3_in, 0)], [(far_2, 0)])
    return out


def regroup_rows(amps, owner_map, tile_size):
    pair_count, virt_count, c_count = amps.shape
    ordered = jnp.take(
        amps.reshape(pair_count, virt_count // tile_size, tile_size, c_count), owner_map, axis=1
    )
    ordered = ordered.reshape(pair_count, virt_count, c_count)
    return lax.all_to_all(ordered, "wide", split_axis=1, concat_axis=0, tiled=True)


def join_halves(amps):
    return lax.all_gather(amps, "sub", axis=2, tiled=True)


def shards(amplitudes, t_mask, integrals, w_mask, owner_map):
    tile_count = owner_map.shape[0]
    pair_here, virt_count, c_here = amplitudes.shape
    tile_size = virt_count // tile_count
    t_scale = t_mask.astype(jnp.bfloat16)
    masked_t = (
        amplitudes.reshape(pair_here, tile_count, tile_size, t_mask.shape[2], tile_size)
        * t_scale[:, :, None, :, None]
    )
    masked_t = masked_t.reshape(pair_here, virt_count, c_here)
    k_count, c_rows, b_cols = integrals.shape
    w_scale = w_mask.astype(jnp.bfloat16)
    masked_w = (
        integrals.reshape(k_count, w_mask.shape[1], tile_size, w_mask.shape[2], tile_size)
        * w_scale[:, :, None, :, None]
    )
    masked_w = masked_w.reshape(k_count, c_rows, b_cols)
    regrouped = join_halves(regroup_rows(masked_t, owner_map, tile_size))
    pair_count, row_count, col_count = regrouped.shape
    occ_count = pair_count // k_count
    blocks = regrouped.reshape(occ_count, k_count, row_count, col_count)
    partial_value = jnp.einsum(
        "ikac,kcb->iab", blocks, masked_w, preferred_element_type=jnp.float32
    )
    rounded = partial_value.astype(jnp.bfloat16)
    return (
        lax.psum_scatter(rounded, "narrow", scatter_dimension=0, tiled=True)
        .astype(jnp.float32)
        .astype(jnp.bfloat16)
    )


def solution(mesh):
    in_specs = (
        P(("group", "wide"), None, ("narrow", "sub")),
        P(("group", "wide"), None, ("narrow", "sub")),
        P("group", "narrow", "sub"),
        P("group", "narrow", "sub"),
        P(),
    )
    out_specs = P(("group", "narrow"), "wide", "sub")
    planes = (mesh.shape["wide"], mesh.shape["narrow"], mesh.shape["sub"]) == (4, 2, 2)
    body = plane_shards if planes else shards
    return jax.shard_map(body, mesh=mesh, in_specs=in_specs, out_specs=out_specs, check_vma=False)
```

```python
import jax
import jax.numpy as jnp
from jax import lax
from jax.experimental import pallas as pl
from jax.experimental.pallas import tpu as pltpu
from jax.sharding import PartitionSpec as P

BF16 = jnp.bfloat16
F32 = jnp.float32
MIB = 2**20

SUM_HOME = [(0, 2), (2, 2), (1, 3)]
SUM_AWAY = [(0, 3), (1, 2), (2, 3), (3, 2)]
SUM_LAST = (3, 3)
NEAR = [(0, 1), (1, 1), (2, 1), (3, 1)]
OWN = [(0, 0), (1, 0), (2, 0), (3, 0)]

ANY = pl.BlockSpec(memory_space=pl.ANY)
COST = pl.CostEstimate(flops=10**12, bytes_accessed=10**9, transcendentals=0)


def pick(values, index):
    chosen = values[0]
    for at, value in enumerate(values[1:], 1):
        chosen = jnp.where(index == at, value, chosen)
    return chosen


def widen(mask, tile_size, tile_dim):
    tiles = mask.shape[tile_dim]
    shape = (tiles, tiles * tile_size)
    column = lax.broadcasted_iota(jnp.int32, shape, 1)
    first = lax.broadcasted_iota(jnp.int32, shape, 0) * tile_size
    spread = (column >= first) & (column < first + tile_size)
    return lax.dot_general(
        mask.astype(F32), spread.astype(F32), (((tile_dim,), (0,)), ((), ())), preferred_element_type=F32
    )


class Chain:
    def __init__(self):
        self.before = None

    def call(
        self, kernel, name, operands, out_shape, grid, in_specs, out_specs, prefetch=(), aliases=None, scratch=()
    ):
        skip = len(prefetch) + len(operands)
        before = self.before
        known = before is None or any(before is operand for operand in operands)
        after = () if known else (before,)

        def body(*refs):
            kernel(*refs[:skip], *refs[skip + len(after):])

        result = pl.pallas_call(
            body,
            out_shape=out_shape,
            grid_spec=pltpu.PrefetchScalarGridSpec(
                num_scalar_prefetch=len(prefetch),
                grid=grid,
                in_specs=[*in_specs, *[ANY] * len(after)],
                out_specs=out_specs,
                scratch_shapes=scratch,
            ),
            input_output_aliases=aliases or {},
            compiler_params=pltpu.CompilerParams(vmem_limit_bytes=64 * MIB),
            cost_estimate=COST,
            name=name,
        )(*prefetch, *operands, *after)
        self.before = result[0] if isinstance(result, (list, tuple)) else result
        return result

    def order_tiles(self, role, owner_map, amps, t_mask, tile_size, blocks):
        c_here = amps.shape[2]
        tiles = owner_map.shape[0] // 4
        rows = tiles * tile_size
        k_count = 2

        def choose(role, g, part):
            home, away = ([pair[at][part] for pair in blocks] for at in (0, 1))
            return pick([h if h == a else jnp.where(role[0] == 1, h, a) for h, a in zip(home, away)], g)

        def tile_of(j, g, role, owner):
            return owner[(role[1] ^ choose(role, g, 1)) * tiles + j]

        def kernel(role, owner, mask_ref, *refs):
            out_ref, wide_ref = refs[-2:]
            g = pl.program_id(0)
            for k in range(k_count):
                wide_ref[k] = widen(mask_ref[k], tile_size, 0)
            for j in range(tiles):
                tile = tile_of(j, g, role, owner)
                for k in range(k_count):
                    scale = wide_ref[k, pl.ds(tile, 1), :].astype(BF16)
                    out_ref[0, pl.ds(j * tile_size, tile_size), pl.ds(k * c_here, c_here)] = refs[j][k] * scale

        def pair(g, role, owner):
            return (choose(role, g, 0), 0, 0)

        in_specs = [pl.BlockSpec((k_count, *t_mask.shape[1:]), pair)]
        for j in range(tiles):
            in_specs.append(
                pl.BlockSpec(
                    (k_count, tile_size, c_here),
                    lambda g, role, owner, j=j: (choose(role, g, 0), tile_of(j, g, role, owner), 0),
                )
            )
        return self.call(
            kernel,
            "order_tiles",
            (t_mask, *([amps] * tiles)),
            jax.ShapeDtypeStruct((len(blocks), rows, k_count * c_here), BF16),
            (len(blocks),),
            in_specs,
            pl.BlockSpec((1, rows, k_count * c_here), lambda g, role, owner: (g, 0, 0)),
            prefetch=(role, owner_map),
            scratch=[pltpu.VMEM((k_count, t_mask.shape[2], c_here), F32)],
        )

    def mask_integrals(self, role, integrals, w_mask, tile_size):
        k_count, c_rows, b_cols = integrals.shape
        half = c_rows // 2
        half_tiles = half // tile_size

        def kernel(role, mask_ref, in_ref, out_ref, wide_ref):
            wide_ref[...] = widen(mask_ref[0], tile_size, 1)
            for j in range(half_tiles):
                at = pl.ds(j * tile_size, tile_size)
                scale = wide_ref[pl.ds((pl.program_id(0) ^ role[2]) * half_tiles + j, 1), :].astype(BF16)
                out_ref[0, at, :] = in_ref[0, at, :] * scale

        return self.call(
            kernel,
            "mask_integrals",
            (w_mask, integrals),
            jax.ShapeDtypeStruct((2, k_count * half, b_cols), BF16),
            (2, k_count),
            [
                pl.BlockSpec((1, *w_mask.shape[1:]), lambda h, k, role: (k, 0, 0)),
                pl.BlockSpec((1, half, b_cols), lambda h, k, role: (k, h ^ role[2], 0)),
            ],
            pl.BlockSpec((1, half, b_cols), lambda h, k, role: (h, k, 0)),
            prefetch=(role,),
            scratch=[pltpu.VMEM((w_mask.shape[1], b_cols), F32)],
        )

    def contract_apart(self, tiles, weights, first, count):
        mine, theirs = tiles
        _, rows, depth = mine.shape
        b_cols = weights.shape[2]
        steps = 2

        def kernel(mine_ref, theirs_ref, weights_ref, *out_refs):
            g = pl.program_id(0)
            total = jnp.dot(mine_ref[0], weights_ref[0], preferred_element_type=F32)
            total += jnp.dot(theirs_ref[0], weights_ref[1], preferred_element_type=F32)
            for at in range(count):

                @pl.when(g == at)
                def _(out_ref=out_refs[at]):
                    out_ref[0] = total.astype(BF16)

        block = pl.BlockSpec((1, rows // steps, depth), lambda g, r: (first + g, r, 0))

        def out_block(at):
            return pl.BlockSpec(
                (1, rows // steps, b_cols),
                lambda g, r: (0, jnp.where(g < at, 0, jnp.where(g > at, steps - 1, r)), 0),
            )

        return self.call(
            kernel,
            "contract_apart",
            (mine, theirs, weights),
            [jax.ShapeDtypeStruct((1, rows, b_cols), BF16)] * count,
            (count, steps),
            [block, block, pl.BlockSpec(weights.shape, lambda g, r: (0, 0, 0))],
            [out_block(at) for at in range(count)],
        )

    def contract(self, role, tiles, weights, first, count=1):
        mine, theirs = tiles
        _, rows, depth = mine.shape
        b_cols = weights.shape[2]
        steps = 2

        def kernel(role, mine_ref, theirs_ref, weights_ref, out_ref):
            total = jnp.dot(mine_ref[0], weights_ref[0], preferred_element_type=F32)
            total += jnp.dot(theirs_ref[0], weights_ref[1], preferred_element_type=F32)
            out_ref[0] = total.astype(BF16)

        block = pl.BlockSpec((1, rows // steps, depth), lambda g, r, role: (first + g, r, 0))
        return self.call(
            kernel,
            "contract",
            (mine, theirs, weights),
            jax.ShapeDtypeStruct((count, rows, b_cols), BF16),
            (count, steps),
            [block, block, pl.BlockSpec(weights.shape, lambda g, r, role: (0, 0, 0))],
            pl.BlockSpec((1, rows // steps, b_cols), lambda g, r, role: (g, r, 0)),
            prefetch=(role,),
        )

    def add(self, sums):
        steps = 2
        count = len(sums)
        _, rows, b_cols = sums[0][0][0].shape

        def kernel(*refs):
            out_ref = refs[-1]
            g = pl.program_id(0)
            for at in range(count):

                @pl.when(g == at)
                def _(left=refs[2 * at], right=refs[2 * at + 1]):
                    out_ref[...] = (left[...].astype(F32) + right[...].astype(F32)).astype(BF16)

        def block(at, index):
            return pl.BlockSpec(
                (1, rows // steps, b_cols),
                lambda g, r: (index, jnp.where(g < at, 0, jnp.where(g > at, steps - 1, r)), 0),
            )

        return self.call(
            kernel,
            "add",
            tuple(array for both in sums for array, _ in both),
            jax.ShapeDtypeStruct((count, rows, b_cols), BF16),
            (count, steps),
            [block(at, index) for at, both in enumerate(sums) for _, index in both],
            pl.BlockSpec((1, rows // steps, b_cols), lambda g, r: (g, r, 0)),
        )

    def hand_on(self, value):
        return self.call(
            lambda *refs: None,
            "hand_on",
            (value,),
            jax.ShapeDtypeStruct(value.shape, value.dtype),
            (1,),
            [ANY],
            ANY,
            aliases={0: 0},
        )

    def place(self, role, out, home_terms, away_terms, blocks=None, block_count=8):
        terms = (*home_terms, *away_terms)
        _, rows, b_cols = terms[0][0].shape
        steps = 2
        orbitals = block_count // 2

        def total(refs):
            if len(refs) == 1:
                return refs[0][...]
            return (refs[0][...].astype(F32) + refs[1][...].astype(F32)).astype(BF16)

        def kernel(role, *refs):
            out_ref = refs[-1]
            split = len(home_terms)

            @pl.when(role[0] == 1)
            def _():
                out_ref[...] = total(refs[:split])

            @pl.when(role[0] == 0)
            def _():
                out_ref[...] = total(refs[split:len(terms)])

        def block(index):
            return pl.BlockSpec((1, rows // steps, b_cols), lambda r, role: (index, r, 0))

        def slot(role):
            if blocks is None:
                return 0
            orbital, distance = (jnp.where(role[0] == 1, *pair) for pair in zip(*blocks))
            return ((role[1] ^ distance) % 2) * orbitals + orbital

        held = () if out is None else (out,)
        return self.call(
            kernel,
            "place",
            (*[array for array, _ in terms], *held),
            jax.ShapeDtypeStruct((block_count, rows, b_cols), BF16),
            (steps,),
            [block(index) for _, index in terms] + [ANY] * len(held),
            pl.BlockSpec((1, rows // steps, b_cols), lambda r, role: (slot(role), r, 0)),
            prefetch=(role,),
            aliases={1 + len(terms): 0} if held else None,
        )


def plane_shards(amplitudes, t_mask, integrals, w_mask, owner_map):
    tile_size = integrals.shape[1] // w_mask.shape[1]
    at_wide = lax.axis_index("wide")
    home = (lax.axis_index("narrow") == at_wide // 2).astype(jnp.int32)
    role = jnp.stack([home, at_wide, lax.axis_index("sub")])
    masks = jnp.swapaxes(t_mask, 1, 2)
    both = ("wide", "narrow")

    def device(w, at_home):
        return w * 2 + (w // 2 if at_home else 1 - w // 2)

    def move(x, pairs):
        return lax.ppermute(x, both, pairs)

    inward = [(device(w, False), device(w, True)) for w in range(4)]
    outward = [(device(w, True), device(w, False)) for w in range(4)]

    def far(home_distance=None, away_distance=None):
        pairs = []
        for w in range(4):
            keeper = device(w, True) % 2
            for at_home, distance in ((True, home_distance), (False, away_distance)):
                if distance is not None:
                    pairs.append((device(w, at_home), keeper + 2 * (w ^ distance)))
        return pairs

    near = [(device(w, True), device(w, True) % 2 + 2 * (w ^ 1)) for w in range(4)]
    chain = Chain()

    def ordered_later(blocks):
        return chain.order_tiles(role, owner_map, amplitudes, masks, tile_size, blocks)

    def exchange(tiles):
        return tiles, lax.ppermute(tiles, "sub", [(0, 1), (1, 0)])

    def ordered(blocks):
        return exchange(ordered_later(blocks))

    def contract(tiles, first, count=1):
        return chain.contract(role, tiles, weights, first, count)

    def add(left, right):
        return chain.add([(left, right)])

    def same(block):
        return (block, block)

    def place(out, home_block, away_block, home_terms, away_terms):
        return chain.place(role, out, home_terms, away_terms, (home_block, away_block))

    swap = inward + outward
    give = [(away, home) for home, away in zip(NEAR, SUM_AWAY)]
    keep = list(zip(NEAR, SUM_AWAY))

    def to_far(at):
        return far(SUM_HOME[at][1], None)

    def round_pairs(at):
        return near + far(None, SUM_AWAY[at][1])

    tiles_a = ordered([give[0], same(SUM_LAST)])
    weights = chain.mask_integrals(role, integrals, w_mask, tile_size)
    tiles_b = ordered([same(SUM_HOME[0]), keep[0]])
    got_0 = move(contract(tiles_a, 0), swap)
    home_0, keep_0 = chain.contract_apart(tiles_b, weights, 0, 2)
    home_0_in = move(home_0, inward)
    last = contract(tiles_a, 1)
    last_away = move(last, far(None, SUM_LAST[1]))
    last_home = move(last, far(SUM_LAST[1], None))
    tiles_c = ordered([give[1], same(SUM_HOME[1]), keep[1], give[2]])

    round_0 = move(add((keep_0, 0), (got_0, 0)), round_pairs(0))
    give_1, home_1 = chain.contract_apart(tiles_c, weights, 0, 2)
    got_1 = move(give_1, swap)
    home_0_in = chain.hand_on(home_0_in)
    home_1 = chain.hand_on(home_1)
    home_1_in = move(home_1, inward)
    keep_1, give_2 = chain.contract_apart(tiles_c, weights, 2, 2)
    tiles_d = ordered_later(
        [same(SUM_HOME[2]), keep[2], give[3], keep[3], *[same(block) for block in OWN]]
    )
    last_away = chain.hand_on(last_away)
    last_home = chain.hand_on(last_home)
    far_0 = move(add((home_0, 0), (home_0_in, 0)), to_far(0))
    tiles_d = exchange(chain.hand_on(tiles_d))

    round_0 = chain.hand_on(round_0)
    round_1 = move(add((keep_1, 0), (got_1, 0)), round_pairs(1))
    got_2 = move(chain.hand_on(give_2), swap)
    home_2, keep_2 = chain.contract_apart(tiles_d, weights, 0, 2)
    home_1_in = chain.hand_on(home_1_in)
    home_2 = chain.hand_on(home_2)
    home_2_in = move(home_2, inward)
    far_0 = chain.hand_on(far_0)
    far_1 = move(add((home_1, 0), (home_1_in, 0)), to_far(1))
    give_3, keep_3 = chain.contract_apart(tiles_d, weights, 2, 2)
    own_012 = contract(tiles_d, 4, 3)

    got_3 = move(chain.hand_on(give_3), swap)
    round_1 = chain.hand_on(round_1)
    round_2 = move(add((keep_2, 0), (got_2, 0)), round_pairs(2))
    home_2_in = chain.hand_on(home_2_in)
    own_012 = chain.hand_on(own_012)
    own_012_in = move(own_012, inward)
    own_3 = contract(tiles_d, 7)
    far_1 = chain.hand_on(far_1)
    far_2 = move(add((home_2, 0), (home_2_in, 0)), to_far(2))
    out = place(None, NEAR[0], SUM_AWAY[0], [(round_0, 0)], [(round_0, 0)])
    out = place(out, NEAR[1], SUM_AWAY[1], [(round_1, 0)], [(round_1, 0)])

    round_2 = chain.hand_on(round_2)
    round_3 = move(add((keep_3, 0), (got_3, 0)), round_pairs(3))
    own_3 = chain.hand_on(own_3)
    own_3_in = move(own_3, inward)
    out = place(out, NEAR[2], SUM_AWAY[2], [(round_2, 0)], [(round_2, 0)])
    far_2 = chain.hand_on(far_2)
    out = place(out, OWN[0], SUM_LAST, [(own_012, 0), (own_012_in, 0)], [(last_away, 0), (last_home, 0)])
    out = place(out, OWN[1], SUM_HOME[0], [(own_012, 1), (own_012_in, 1)], [(far_0, 0)])
    out = place(out, OWN[2], SUM_HOME[1], [(own_012, 2), (own_012_in, 2)], [(far_1, 0)])
    out = place(out, NEAR[3], SUM_AWAY[3], [(round_3, 0)], [(round_3, 0)])
    out = place(out, OWN[3], SUM_HOME[2], [(own_3, 0), (own_3_in, 0)], [(far_2, 0)])
    return out


def regroup_rows(amps, owner_map, tile_size):
    pair_count, virt_count, c_count = amps.shape
    ordered = jnp.take(
        amps.reshape(pair_count, virt_count // tile_size, tile_size, c_count), owner_map, axis=1
    )
    ordered = ordered.reshape(pair_count, virt_count, c_count)
    return lax.all_to_all(ordered, "wide", split_axis=1, concat_axis=0, tiled=True)


def join_halves(amps):
    return lax.all_gather(amps, "sub", axis=2, tiled=True)


def shards(amplitudes, t_mask, integrals, w_mask, owner_map):
    tile_count = owner_map.shape[0]
    pair_here, virt_count, c_here = amplitudes.shape
    tile_size = virt_count // tile_count
    t_scale = t_mask.astype(jnp.bfloat16)
    masked_t = (
        amplitudes.reshape(pair_here, tile_count, tile_size, t_mask.shape[2], tile_size)
        * t_scale[:, :, None, :, None]
    )
    masked_t = masked_t.reshape(pair_here, virt_count, c_here)
    k_count, c_rows, b_cols = integrals.shape
    w_scale = w_mask.astype(jnp.bfloat16)
    masked_w = (
        integrals.reshape(k_count, w_mask.shape[1], tile_size, w_mask.shape[2], tile_size)
        * w_scale[:, :, None, :, None]
    )
    masked_w = masked_w.reshape(k_count, c_rows, b_cols)
    regrouped = join_halves(regroup_rows(masked_t, owner_map, tile_size))
    pair_count, row_count, col_count = regrouped.shape
    occ_count = pair_count // k_count
    blocks = regrouped.reshape(occ_count, k_count, row_count, col_count)
    partial_value = jnp.einsum(
        "ikac,kcb->iab", blocks, masked_w, preferred_element_type=jnp.float32
    )
    rounded = partial_value.astype(jnp.bfloat16)
    return (
        lax.psum_scatter(rounded, "narrow", scatter_dimension=0, tiled=True)
        .astype(jnp.float32)
        .astype(jnp.bfloat16)
    )


def solution(mesh):
    in_specs = (
        P(("group", "wide"), None, ("narrow", "sub")),
        P(("group", "wide"), None, ("narrow", "sub")),
        P("group", "narrow", "sub"),
        P("group", "narrow", "sub"),
        P(),
    )
    out_specs = P(("group", "narrow"), "wide", "sub")
    planes = (mesh.shape["wide"], mesh.shape["narrow"], mesh.shape["sub"]) == (4, 2, 2)
    body = plane_shards if planes else shards
    return jax.shard_map(body, mesh=mesh, in_specs=in_specs, out_specs=out_specs, check_vma=False)
```

```python
import jax
import jax.numpy as jnp
from jax import lax
from jax.experimental import pallas as pl
from jax.experimental.pallas import tpu as pltpu
from jax.sharding import PartitionSpec as P

BF16 = jnp.bfloat16
F32 = jnp.float32
MIB = 2**20

SUM_HOME = [(0, 2), (2, 2), (1, 3)]
SUM_AWAY = [(0, 3), (1, 2), (2, 3), (3, 2)]
SUM_LAST = (3, 3)
NEAR = [(0, 1), (1, 1), (2, 1), (3, 1)]
OWN = [(0, 0), (1, 0), (2, 0), (3, 0)]

ANY = pl.BlockSpec(memory_space=pl.ANY)
COST = pl.CostEstimate(flops=10**12, bytes_accessed=10**9, transcendentals=0)


def pick(values, index):
    chosen = values[0]
    for at, value in enumerate(values[1:], 1):
        chosen = jnp.where(index == at, value, chosen)
    return chosen


def widen(mask, tile_size, tile_dim):
    tiles = mask.shape[tile_dim]
    shape = (tiles, tiles * tile_size)
    column = lax.broadcasted_iota(jnp.int32, shape, 1)
    first = lax.broadcasted_iota(jnp.int32, shape, 0) * tile_size
    spread = (column >= first) & (column < first + tile_size)
    return lax.dot_general(
        mask.astype(F32), spread.astype(F32), (((tile_dim,), (0,)), ((), ())), preferred_element_type=F32
    )


class Chain:
    def __init__(self):
        self.before = None

    def call(
        self, kernel, name, operands, out_shape, grid, in_specs, out_specs, prefetch=(), aliases=None, scratch=()
    ):
        skip = len(prefetch) + len(operands)
        before = self.before
        known = before is None or any(before is operand for operand in operands)
        after = () if known else (before,)

        def body(*refs):
            kernel(*refs[:skip], *refs[skip + len(after):])

        result = pl.pallas_call(
            body,
            out_shape=out_shape,
            grid_spec=pltpu.PrefetchScalarGridSpec(
                num_scalar_prefetch=len(prefetch),
                grid=grid,
                in_specs=[*in_specs, *[ANY] * len(after)],
                out_specs=out_specs,
                scratch_shapes=scratch,
            ),
            input_output_aliases=aliases or {},
            compiler_params=pltpu.CompilerParams(vmem_limit_bytes=64 * MIB),
            cost_estimate=COST,
            name=name,
        )(*prefetch, *operands, *after)
        self.before = result[0] if isinstance(result, (list, tuple)) else result
        return result

    def order_tiles(self, role, owner_map, amps, t_mask, tile_size, blocks):
        c_here = amps.shape[2]
        tiles = owner_map.shape[0] // 4
        rows = tiles * tile_size
        k_count = 2

        def choose(role, g, part):
            home, away = ([pair[at][part] for pair in blocks] for at in (0, 1))
            return pick([h if h == a else jnp.where(role[0] == 1, h, a) for h, a in zip(home, away)], g)

        def tile_of(j, g, role, owner):
            return owner[(role[1] ^ choose(role, g, 1)) * tiles + j]

        def kernel(role, owner, mask_ref, *refs):
            out_ref, wide_ref = refs[-2:]
            g = pl.program_id(0)
            for k in range(k_count):
                wide_ref[k] = widen(mask_ref[k], tile_size, 0)
            for j in range(tiles):
                tile = tile_of(j, g, role, owner)
                for k in range(k_count):
                    scale = wide_ref[k, pl.ds(tile, 1), :].astype(BF16)
                    out_ref[0, pl.ds(j * tile_size, tile_size), pl.ds(k * c_here, c_here)] = refs[j][k] * scale

        def pair(g, role, owner):
            return (choose(role, g, 0), 0, 0)

        in_specs = [pl.BlockSpec((k_count, *t_mask.shape[1:]), pair)]
        for j in range(tiles):
            in_specs.append(
                pl.BlockSpec(
                    (k_count, tile_size, c_here),
                    lambda g, role, owner, j=j: (choose(role, g, 0), tile_of(j, g, role, owner), 0),
                )
            )
        return self.call(
            kernel,
            "order_tiles",
            (t_mask, *([amps] * tiles)),
            jax.ShapeDtypeStruct((len(blocks), rows, k_count * c_here), BF16),
            (len(blocks),),
            in_specs,
            pl.BlockSpec((1, rows, k_count * c_here), lambda g, role, owner: (g, 0, 0)),
            prefetch=(role, owner_map),
            scratch=[pltpu.VMEM((k_count, t_mask.shape[2], c_here), F32)],
        )

    def mask_integrals(self, role, integrals, w_mask, tile_size):
        k_count, c_rows, b_cols = integrals.shape
        half = c_rows // 2
        half_tiles = half // tile_size

        def kernel(role, mask_ref, in_ref, out_ref, wide_ref):
            wide_ref[...] = widen(mask_ref[0], tile_size, 1)
            for j in range(half_tiles):
                at = pl.ds(j * tile_size, tile_size)
                scale = wide_ref[pl.ds((pl.program_id(0) ^ role[2]) * half_tiles + j, 1), :].astype(BF16)
                out_ref[0, at, :] = in_ref[0, at, :] * scale

        return self.call(
            kernel,
            "mask_integrals",
            (w_mask, integrals),
            jax.ShapeDtypeStruct((2, k_count * half, b_cols), BF16),
            (2, k_count),
            [
                pl.BlockSpec((1, *w_mask.shape[1:]), lambda h, k, role: (k, 0, 0)),
                pl.BlockSpec((1, half, b_cols), lambda h, k, role: (k, h ^ role[2], 0)),
            ],
            pl.BlockSpec((1, half, b_cols), lambda h, k, role: (h, k, 0)),
            prefetch=(role,),
            scratch=[pltpu.VMEM((w_mask.shape[1], b_cols), F32)],
        )

    def contract_apart(self, tiles, weights, first, count):
        mine, theirs = tiles
        _, rows, depth = mine.shape
        b_cols = weights.shape[2]
        steps = 2

        def kernel(mine_ref, theirs_ref, weights_ref, *out_refs):
            g = pl.program_id(0)
            total = jnp.dot(mine_ref[0], weights_ref[0], preferred_element_type=F32)
            total += jnp.dot(theirs_ref[0], weights_ref[1], preferred_element_type=F32)
            for at in range(count):

                @pl.when(g == at)
                def _(out_ref=out_refs[at]):
                    out_ref[0] = total.astype(BF16)

        block = pl.BlockSpec((1, rows // steps, depth), lambda g, r: (first + g, r, 0))

        def out_block(at):
            return pl.BlockSpec(
                (1, rows // steps, b_cols),
                lambda g, r: (0, jnp.where(g < at, 0, jnp.where(g > at, steps - 1, r)), 0),
            )

        return self.call(
            kernel,
            "contract_apart",
            (mine, theirs, weights),
            [jax.ShapeDtypeStruct((1, rows, b_cols), BF16)] * count,
            (count, steps),
            [block, block, pl.BlockSpec(weights.shape, lambda g, r: (0, 0, 0))],
            [out_block(at) for at in range(count)],
        )

    def contract(self, role, tiles, weights, first, count=1):
        mine, theirs = tiles
        _, rows, depth = mine.shape
        b_cols = weights.shape[2]
        steps = 2

        def kernel(role, mine_ref, theirs_ref, weights_ref, out_ref):
            total = jnp.dot(mine_ref[0], weights_ref[0], preferred_element_type=F32)
            total += jnp.dot(theirs_ref[0], weights_ref[1], preferred_element_type=F32)
            out_ref[0] = total.astype(BF16)

        block = pl.BlockSpec((1, rows // steps, depth), lambda g, r, role: (first + g, r, 0))
        return self.call(
            kernel,
            "contract",
            (mine, theirs, weights),
            jax.ShapeDtypeStruct((count, rows, b_cols), BF16),
            (count, steps),
            [block, block, pl.BlockSpec(weights.shape, lambda g, r, role: (0, 0, 0))],
            pl.BlockSpec((1, rows // steps, b_cols), lambda g, r, role: (g, r, 0)),
            prefetch=(role,),
        )

    def add(self, sums):
        steps = 2
        count = len(sums)
        _, rows, b_cols = sums[0][0][0].shape

        def kernel(*refs):
            out_ref = refs[-1]
            g = pl.program_id(0)
            for at in range(count):

                @pl.when(g == at)
                def _(left=refs[2 * at], right=refs[2 * at + 1]):
                    out_ref[...] = (left[...].astype(F32) + right[...].astype(F32)).astype(BF16)

        def block(at, index):
            return pl.BlockSpec(
                (1, rows // steps, b_cols),
                lambda g, r: (index, jnp.where(g < at, 0, jnp.where(g > at, steps - 1, r)), 0),
            )

        return self.call(
            kernel,
            "add",
            tuple(array for both in sums for array, _ in both),
            jax.ShapeDtypeStruct((count, rows, b_cols), BF16),
            (count, steps),
            [block(at, index) for at, both in enumerate(sums) for _, index in both],
            pl.BlockSpec((1, rows // steps, b_cols), lambda g, r: (g, r, 0)),
        )

    def hand_on(self, value):
        return self.call(
            lambda *refs: None,
            "hand_on",
            (value,),
            jax.ShapeDtypeStruct(value.shape, value.dtype),
            (1,),
            [ANY],
            ANY,
            aliases={0: 0},
        )

    def place(self, role, out, home_terms, away_terms, blocks=None, block_count=8):
        terms = (*home_terms, *away_terms)
        _, rows, b_cols = terms[0][0].shape
        steps = 2
        orbitals = block_count // 2

        def total(refs):
            if len(refs) == 1:
                return refs[0][...]
            return (refs[0][...].astype(F32) + refs[1][...].astype(F32)).astype(BF16)

        def kernel(role, *refs):
            out_ref = refs[-1]
            split = len(home_terms)

            @pl.when(role[0] == 1)
            def _():
                out_ref[...] = total(refs[:split])

            @pl.when(role[0] == 0)
            def _():
                out_ref[...] = total(refs[split:len(terms)])

        def block(index):
            return pl.BlockSpec((1, rows // steps, b_cols), lambda r, role: (index, r, 0))

        def slot(role):
            if blocks is None:
                return 0
            orbital, distance = (jnp.where(role[0] == 1, *pair) for pair in zip(*blocks))
            return ((role[1] ^ distance) % 2) * orbitals + orbital

        held = () if out is None else (out,)
        return self.call(
            kernel,
            "place",
            (*[array for array, _ in terms], *held),
            jax.ShapeDtypeStruct((block_count, rows, b_cols), BF16),
            (steps,),
            [block(index) for _, index in terms] + [ANY] * len(held),
            pl.BlockSpec((1, rows // steps, b_cols), lambda r, role: (slot(role), r, 0)),
            prefetch=(role,),
            aliases={1 + len(terms): 0} if held else None,
        )


def plane_shards(amplitudes, t_mask, integrals, w_mask, owner_map):
    tile_size = integrals.shape[1] // w_mask.shape[1]
    at_wide = lax.axis_index("wide")
    home = (lax.axis_index("narrow") == at_wide // 2).astype(jnp.int32)
    role = jnp.stack([home, at_wide, lax.axis_index("sub")])
    masks = jnp.swapaxes(t_mask, 1, 2)
    both = ("wide", "narrow")

    def device(w, at_home):
        return w * 2 + (w // 2 if at_home else 1 - w // 2)

    def move(x, pairs):
        return lax.ppermute(x, both, pairs)

    inward = [(device(w, False), device(w, True)) for w in range(4)]
    outward = [(device(w, True), device(w, False)) for w in range(4)]

    def far(home_distance=None, away_distance=None):
        pairs = []
        for w in range(4):
            keeper = device(w, True) % 2
            for at_home, distance in ((True, home_distance), (False, away_distance)):
                if distance is not None:
                    pairs.append((device(w, at_home), keeper + 2 * (w ^ distance)))
        return pairs

    near = [(device(w, True), device(w, True) % 2 + 2 * (w ^ 1)) for w in range(4)]
    chain = Chain()

    def ordered_later(blocks):
        return chain.order_tiles(role, owner_map, amplitudes, masks, tile_size, blocks)

    def exchange(tiles):
        return tiles, lax.ppermute(tiles, "sub", [(0, 1), (1, 0)])

    def ordered(blocks):
        return exchange(ordered_later(blocks))

    def contract(tiles, first, count=1):
        return chain.contract(role, tiles, weights, first, count)

    def add(left, right):
        return chain.add([(left, right)])

    def same(block):
        return (block, block)

    def place(out, home_block, away_block, home_terms, away_terms):
        return chain.place(role, out, home_terms, away_terms, (home_block, away_block))

    swap = inward + outward
    give = [(away, home) for home, away in zip(NEAR, SUM_AWAY)]
    keep = list(zip(NEAR, SUM_AWAY))

    def to_far(at):
        return far(SUM_HOME[at][1], None)

    def round_pairs(at):
        return near + far(None, SUM_AWAY[at][1])

    tiles_a = ordered([give[0], same(SUM_LAST)])
    weights = chain.mask_integrals(role, integrals, w_mask, tile_size)
    tiles_b = ordered([same(SUM_HOME[0]), keep[0]])
    got_0 = move(contract(tiles_a, 0), swap)
    home_0, keep_0 = chain.contract_apart(tiles_b, weights, 0, 2)
    home_0_in = move(home_0, inward)
    last = contract(tiles_a, 1)
    last_away = move(last, far(None, SUM_LAST[1]))
    last_home = move(last, far(SUM_LAST[1], None))
    tiles_c = ordered([give[1], same(SUM_HOME[1]), keep[1], give[2]])

    round_0 = move(add((keep_0, 0), (got_0, 0)), round_pairs(0))
    give_1, home_1 = chain.contract_apart(tiles_c, weights, 0, 2)
    got_1 = move(give_1, swap)
    home_0_in = chain.hand_on(home_0_in)
    home_1 = chain.hand_on(home_1)
    home_1_in = move(home_1, inward)
    keep_1, give_2 = chain.contract_apart(tiles_c, weights, 2, 2)
    tiles_d = ordered_later(
        [same(SUM_HOME[2]), keep[2], give[3], keep[3], *[same(block) for block in OWN]]
    )
    last_away = chain.hand_on(last_away)
    last_home = chain.hand_on(last_home)
    far_0 = move(add((home_0, 0), (home_0_in, 0)), to_far(0))
    tiles_d = exchange(chain.hand_on(tiles_d))

    got_2 = move(chain.hand_on(give_2), swap)
    round_0 = chain.hand_on(round_0)
    round_1 = move(add((keep_1, 0), (got_1, 0)), round_pairs(1))
    home_2, keep_2 = chain.contract_apart(tiles_d, weights, 0, 2)
    home_1_in = chain.hand_on(home_1_in)
    home_2 = chain.hand_on(home_2)
    home_2_in = move(home_2, inward)
    far_0 = chain.hand_on(far_0)
    far_1 = move(add((home_1, 0), (home_1_in, 0)), to_far(1))
    give_3, keep_3 = chain.contract_apart(tiles_d, weights, 2, 2)
    own_012 = contract(tiles_d, 4, 3)

    got_3 = move(chain.hand_on(give_3), swap)
    round_1 = chain.hand_on(round_1)
    round_2 = move(add((keep_2, 0), (got_2, 0)), round_pairs(2))
    home_2_in = chain.hand_on(home_2_in)
    own_012 = chain.hand_on(own_012)
    own_012_in = move(own_012, inward)
    own_3 = contract(tiles_d, 7)
    far_1 = chain.hand_on(far_1)
    far_2 = move(add((home_2, 0), (home_2_in, 0)), to_far(2))
    out = place(None, NEAR[0], SUM_AWAY[0], [(round_0, 0)], [(round_0, 0)])
    out = place(out, NEAR[1], SUM_AWAY[1], [(round_1, 0)], [(round_1, 0)])

    round_2 = chain.hand_on(round_2)
    round_3 = move(add((keep_3, 0), (got_3, 0)), round_pairs(3))
    own_3 = chain.hand_on(own_3)
    own_3_in = move(own_3, inward)
    out = place(out, NEAR[2], SUM_AWAY[2], [(round_2, 0)], [(round_2, 0)])
    far_2 = chain.hand_on(far_2)
    out = place(out, OWN[0], SUM_LAST, [(own_012, 0), (own_012_in, 0)], [(last_away, 0), (last_home, 0)])
    out = place(out, OWN[1], SUM_HOME[0], [(own_012, 1), (own_012_in, 1)], [(far_0, 0)])
    out = place(out, OWN[2], SUM_HOME[1], [(own_012, 2), (own_012_in, 2)], [(far_1, 0)])
    out = place(out, NEAR[3], SUM_AWAY[3], [(round_3, 0)], [(round_3, 0)])
    out = place(out, OWN[3], SUM_HOME[2], [(own_3, 0), (own_3_in, 0)], [(far_2, 0)])
    return out


def regroup_rows(amps, owner_map, tile_size):
    pair_count, virt_count, c_count = amps.shape
    ordered = jnp.take(
        amps.reshape(pair_count, virt_count // tile_size, tile_size, c_count), owner_map, axis=1
    )
    ordered = ordered.reshape(pair_count, virt_count, c_count)
    return lax.all_to_all(ordered, "wide", split_axis=1, concat_axis=0, tiled=True)


def join_halves(amps):
    return lax.all_gather(amps, "sub", axis=2, tiled=True)


def shards(amplitudes, t_mask, integrals, w_mask, owner_map):
    tile_count = owner_map.shape[0]
    pair_here, virt_count, c_here = amplitudes.shape
    tile_size = virt_count // tile_count
    t_scale = t_mask.astype(jnp.bfloat16)
    masked_t = (
        amplitudes.reshape(pair_here, tile_count, tile_size, t_mask.shape[2], tile_size)
        * t_scale[:, :, None, :, None]
    )
    masked_t = masked_t.reshape(pair_here, virt_count, c_here)
    k_count, c_rows, b_cols = integrals.shape
    w_scale = w_mask.astype(jnp.bfloat16)
    masked_w = (
        integrals.reshape(k_count, w_mask.shape[1], tile_size, w_mask.shape[2], tile_size)
        * w_scale[:, :, None, :, None]
    )
    masked_w = masked_w.reshape(k_count, c_rows, b_cols)
    regrouped = join_halves(regroup_rows(masked_t, owner_map, tile_size))
    pair_count, row_count, col_count = regrouped.shape
    occ_count = pair_count // k_count
    blocks = regrouped.reshape(occ_count, k_count, row_count, col_count)
    partial_value = jnp.einsum(
        "ikac,kcb->iab", blocks, masked_w, preferred_element_type=jnp.float32
    )
    rounded = partial_value.astype(jnp.bfloat16)
    return (
        lax.psum_scatter(rounded, "narrow", scatter_dimension=0, tiled=True)
        .astype(jnp.float32)
        .astype(jnp.bfloat16)
    )


def solution(mesh):
    in_specs = (
        P(("group", "wide"), None, ("narrow", "sub")),
        P(("group", "wide"), None, ("narrow", "sub")),
        P("group", "narrow", "sub"),
        P("group", "narrow", "sub"),
        P(),
    )
    out_specs = P(("group", "narrow"), "wide", "sub")
    planes = (mesh.shape["wide"], mesh.shape["narrow"], mesh.shape["sub"]) == (4, 2, 2)
    body = plane_shards if planes else shards
    return jax.shard_map(body, mesh=mesh, in_specs=in_specs, out_specs=out_specs, check_vma=False)
```
